32 devices in a mesh: groups: 2 (over x), layer: 16 (over z, y, core).
Axes of the slice: x: 2, y: 2, z: 4, core: 2. Of those that a mesh axis runs over, the one named last changes fastest.
Arguments:
- inputs: bfloat16 [1024, 3584], P('groups'), parts along dimension 0, may hold values from -6 to 6
- targets: bfloat16 [1024, 2, 3584], P(('groups', 'layer')), parts along dimension 0, may hold values from -6 to 6
- w_enc: bfloat16 [3584, 16384], P(None, 'layer'), may hold values from -0.09375 to 0.09375
- b_enc: float32 [16384], P('layer'), may hold values from -3 to 3
- w_dec: bfloat16 [16384, 2, 3584], P('layer'), may hold values from -0.09375 to 0.09375
- active_tiles: int32 [32], replicated, may hold values from 0 to 127, as said below
Outputs:
- grad_enc: bfloat16 [7168, 16384], P('groups', 'layer'), parts along dimension 0
- grad_bias: float32 [32768], P(('groups', 'layer')), parts along dimension 0
- grad_dec: bfloat16 [32768, 2, 3584], P(('groups', 'layer')), parts along dimension 0
The draws below stay inside these ranges and needn't reach their ends.
There are 2 independent parts, one for each index of `groups`. The reference program is written for one: setup_inputs(seed, part) draws one part's arguments, and reference() takes and returns one part's arrays. A program takes and returns all parts, laid end to end along the dimension named above; an argument that names none is the same for every part. Nothing has to cross between parts.
Inputs may be any that keep to these rules, and one draw needn't show every extreme that they name: `active_tiles`: 32 distinct block numbers; blocks 0 and 127 are always among them.
All inputs are finite; a program needn't handle non-finite values.
Results may differ from the reference program's by a relative error of at most 0.008.
Values may be sent and summed in bfloat16 or wider, within the bound.
A program may use at most 192 MiB of HBM per device.

```python
import math
import jax
import jax.numpy as jnp
from jax import lax

D = 3584
F = 16384
TILE = 128
TARGETS = 2
TOKENS = 512
TILES = 128
ACTIVE = 32


def draw_active_tiles(key, part):
    key = jax.random.fold_in(key, 7)
    middle = jax.random.permutation(key, TILES - 2) + 1
    ends = jnp.array([0, TILES - 1], dtype=jnp.int32)
    return jnp.concatenate([ends, middle[:ACTIVE - 2].astype(jnp.int32)])


def levels(own_key, extent, pieces, low, top_value):
    level = 1.0
    for position, blocks in pieces:
        heights = jax.random.uniform(jax.random.fold_in(jax.random.fold_in(own_key, 6), position), (blocks,), jnp.float32, low / len(pieces), top_value / len(pieces))
        level = level * jnp.repeat(jnp.exp(heights), extent[position] // blocks).reshape((-1,) + (1,) * (len(extent) - 1 - position))
    return level


def centred(rng, dims, deviation, most, cuts=(), held_as=jnp.bfloat16):
    factor_of = levels(rng, dims, cuts, -0.22, 0.18) if cuts else 1.0
    result = jax.random.normal(rng, dims, jnp.float32) * deviation * factor_of
    return jnp.minimum(jnp.maximum(result, -most), most).astype(held_as)


def setup_inputs(seed: int = 0, part: int = 0) -> dict:
    key_of = jax.random.split(jax.random.key(seed), 7)
    part_keys = jax.random.split(jax.random.fold_in(key_of[6], part), 7)
    return {
        "inputs": centred(part_keys[0], (TOKENS, D), 1.0, 6.0),
        "targets": centred(part_keys[1], (TOKENS, TARGETS, D), 1.0, 6.0, ((0, 16),)),
        "w_enc": centred(key_of[2], (D, F), D ** -0.5, 0.09375, ((1, 16),)),
        "b_enc": centred(key_of[3], (F,), 0.5, 3.0, ((0, 16),), jnp.float32),
        "w_dec": centred(key_of[4], (F, TARGETS, D), (ACTIVE * TILE) ** -0.5, 0.09375, ((0, 16),)),
        "active_tiles": draw_active_tiles(jax.random.fold_in(key_of[6], 71), part),
    }


def reference(inputs, targets, w_enc, b_enc, w_dec, active_tiles):
    tile_ids = jnp.arange(TILES, dtype=jnp.int32)
    tile_on = jnp.any(active_tiles[:, None] == tile_ids[None, :], axis=0)
    fmask = jnp.repeat(tile_on, TILE).astype(jnp.float32)
    pre = jnp.dot(inputs, w_enc, preferred_element_type=jnp.float32) + b_enc
    feats = (jnp.maximum(pre, 0.0) * fmask).astype(jnp.bfloat16)
    w_flat = w_dec.reshape(F, TARGETS * D)
    recon = jnp.dot(feats, w_flat, preferred_element_type=jnp.float32)
    err = (recon - targets.reshape(TOKENS, TARGETS * D).astype(jnp.float32)).astype(jnp.bfloat16)
    scale = 1.0 / math.sqrt(TOKENS)
    grad_dec = (jnp.dot(feats.T, err, preferred_element_type=jnp.float32) * scale).astype(jnp.bfloat16)
    gfeat = jnp.dot(err, w_flat.T, preferred_element_type=jnp.float32) * (feats > 0)
    grad_bias = lax.optimization_barrier(jnp.sum(gfeat, axis=0)) * scale
    grad_enc = (jnp.dot(inputs.T, gfeat.astype(jnp.bfloat16), preferred_element_type=jnp.float32) * scale).astype(jnp.bfloat16)
    return (grad_enc, grad_bias, grad_dec.reshape(F, TARGETS, D))
```

```python
import functools
import math

import jax
import jax.numpy as jnp
from jax import lax
from jax.experimental import pallas as pl
from jax.experimental.pallas import tpu as pltpu
from jax.sharding import PartitionSpec as P

TILE = 128
ZN, YN, CN = 4, 2, 2
PEERS = 5
CORE, YRS, ZRS, ZAG, YAG, CAG, KINDS = 0, 1, 2, 5, 8, 9, 10
LAG = (1, 3, 5, 7, 9, 10)


def exchange_kernel(
    chunks, feats, w_hbm, tgt, out, wbuf, part, r_core, r_y, r_z, w_sem, send, recv
):
    me = lax.axis_index("layer")
    z, y, c = me // 4, (me // 2) % 2, me % 2
    rows = tgt.shape[0]
    quad, half = ZN * rows, YN * ZN * rows
    width = w_hbm.shape[1] // chunks
    core_peer = z * 4 + y * 2 + (1 - c)
    y_peer = z * 4 + (1 - y) * 2 + c
    z_of = [(z + d) % ZN for d in range(1, ZN)]
    z_from = [(z + ZN - d) % ZN for d in range(1, ZN)]
    z_peer = [zz * 4 + y * 2 + c for zz in z_of]

    def at(k):
        return pl.ds(pl.multiple_of(k * width, 128), width)

    def span(start, size):
        return pl.ds(pl.multiple_of(start, 32), size)

    own_half, far_half = span(c * half, half), span((1 - c) * half, half)
    own_quad = span(c * half + y * quad, quad)
    far_quad = span(c * half + (1 - y) * quad, quad)
    own = span(c * half + y * quad + z * rows, rows)

    def of_z(zz):
        return span(c * half + y * quad + zz * rows, rows)

    def copy(src, dst, kind, k, peer):
        return pltpu.make_async_remote_copy(
            src_ref=src,
            dst_ref=dst,
            send_sem=send.at[kind, k],
            recv_sem=recv.at[kind, k],
            device_id={"layer": peer},
            device_id_type=pl.DeviceIdType.MESH,
        )

    def load(k):
        return pltpu.make_async_copy(w_hbm.at[:, at(k)], wbuf.at[:, at(k)], w_sem.at[k])

    def core_copy(k):
        return copy(part.at[far_half, at(k)], r_core.at[:, at(k)], CORE, k, core_peer)

    def y_copy(k):
        return copy(part.at[far_quad, at(k)], r_y.at[:, at(k)], YRS, k, y_peer)

    def z_copy(k, d):
        return copy(part.at[of_z(z_of[d]), at(k)], r_z.at[d, :, at(k)], ZRS + d, k, z_peer[d])

    def z_send(k, d):
        return copy(out.at[own, at(k)], out.at[own, at(k)], ZAG + d, k, z_peer[d])

    def z_take(k, d):
        got = out.at[of_z(z_from[d]), at(k)]
        return copy(got, got, ZAG + d, k, z_peer[d])

    def y_send(k):
        return copy(out.at[own_quad, at(k)], out.at[own_quad, at(k)], YAG, k, y_peer)

    def y_take(k):
        got = out.at[far_quad, at(k)]
        return copy(got, got, YAG, k, y_peer)

    def core_send(k):
        return copy(out.at[own_half, at(k)], out.at[own_half, at(k)], CAG, k, core_peer)

    def core_take(k):
        got = out.at[far_half, at(k)]
        return copy(got, got, CAG, k, core_peer)

    barrier = pltpu.get_barrier_semaphore()
    for peer in (core_peer, y_peer, *z_peer):
        pl.semaphore_signal(
            barrier, inc=1, device_id={"layer": peer}, device_id_type=pl.DeviceIdType.MESH
        )

    @pl.loop(0, chunks)
    def _(k):
        load(k).start()

    pl.semaphore_wait(barrier, PEERS)

    @pl.loop(0, chunks + LAG[-1])
    def _(s):
        @pl.when(s < chunks)
        def _():
            k = s
            load(k).wait()
            part[:, at(k)] = jnp.dot(
                feats[...], wbuf[:, at(k)], preferred_element_type=jnp.float32
            ).astype(jnp.bfloat16)
            core_copy(k).start()

        def stage(lag, body):
            @pl.when((s >= lag) & (s < lag + chunks))
            def _():
                body(s - lag)

        def after_core(k):
            core_copy(k).wait_recv()
            part[own_half, at(k)] = (
                part[own_half, at(k)].astype(jnp.float32) + r_core[:, at(k)].astype(jnp.float32)
            ).astype(jnp.bfloat16)
            y_copy(k).start()

        def after_y(k):
            y_copy(k).wait_recv()
            part[own_quad, at(k)] = (
                part[own_quad, at(k)].astype(jnp.float32) + r_y[:, at(k)].astype(jnp.float32)
            ).astype(jnp.bfloat16)
            for d in range(ZN - 1):
                z_copy(k, d).start()

        def after_z(k):
            total = part[own, at(k)].astype(jnp.float32)
            for d in range(ZN - 1):
                z_copy(k, d).wait_recv()
                total += r_z[d, :, at(k)].astype(jnp.float32)
            out[own, at(k)] = (total - tgt[:, at(k)].astype(jnp.float32)).astype(jnp.bfloat16)
            for d in range(ZN - 1):
                z_send(k, d).start()

        def after_zag(k):
            for d in range(ZN - 1):
                z_take(k, d).wait_recv()
            y_send(k).start()

        def after_yag(k):
            y_take(k).wait_recv()
            core_send(k).start()

        def after_cag(k):
            core_take(k).wait_recv()

        for lag, body in zip(
            LAG, (after_core, after_y, after_z, after_zag, after_yag, after_cag)
        ):
            stage(lag, body)

    @pl.loop(0, chunks)
    def _(k):
        core_copy(k).wait_send()
        y_copy(k).wait_send()
        for d in range(ZN - 1):
            z_copy(k, d).wait_send()
            z_send(k, d).wait_send()
        y_send(k).wait_send()
        core_send(k).wait_send()


def exchange(feats, w_flat, tgt):
    tokens, depth = feats.shape
    columns = w_flat.shape[1]
    rows = tgt.shape[0]
    chunks = 8
    return pl.pallas_call(
        functools.partial(exchange_kernel, chunks),
        out_shape=jax.ShapeDtypeStruct((tokens, columns), jnp.bfloat16),
        in_specs=[
            pl.BlockSpec(memory_space=pltpu.VMEM),
            pl.BlockSpec(memory_space=pl.ANY),
            pl.BlockSpec(memory_space=pltpu.VMEM),
        ],
        out_specs=pl.BlockSpec(memory_space=pltpu.VMEM),
        scratch_shapes=[
            pltpu.VMEM((depth, columns), jnp.bfloat16),
            pltpu.VMEM((tokens, columns), jnp.bfloat16),
            pltpu.VMEM((tokens // CN, columns), jnp.bfloat16),
            pltpu.VMEM((tokens // CN // YN, columns), jnp.bfloat16),
            pltpu.VMEM((ZN - 1, rows, columns), jnp.bfloat16),
            pltpu.SemaphoreType.DMA((chunks,)),
            pltpu.SemaphoreType.DMA((KINDS, chunks)),
            pltpu.SemaphoreType.DMA((KINDS, chunks)),
        ],
        compiler_params=pltpu.CompilerParams(
            collective_id=0, has_side_effects=True, vmem_limit_bytes=56 * 2**20
        ),
        cost_estimate=pl.CostEstimate(
            flops=2 * tokens * depth * columns,
            bytes_accessed=2 * (depth + tokens) * columns,
            transcendentals=0,
        ),
    )(feats, w_flat, tgt)


def by_owner(a, back=False):
    rows = a.shape[0] // (ZN * YN * CN)
    dims = (CN, YN, ZN) if back else (ZN, YN, CN)
    return a.reshape(*dims, rows, -1).transpose(2, 1, 0, 3, 4).reshape(a.shape)


def local(inputs, targets, w_enc, b_enc, w_dec, active_tiles, layers):
    total = inputs.shape[0]
    tok_rows = targets.shape[0]
    feat_dev = w_enc.shape[1]
    scale = 1.0 / math.sqrt(total)
    tiles_dev = feat_dev // TILE
    local_ids = lax.axis_index("layer") * tiles_dev + jnp.arange(tiles_dev, dtype=jnp.int32)
    tile_on = jnp.any(active_tiles[:, None] == local_ids[None, :], axis=0)
    fmask = jnp.repeat(tile_on, TILE).astype(jnp.float32)
    own = layers == ZN * YN * CN
    pre = jnp.dot(inputs, w_enc, preferred_element_type=jnp.float32) + b_enc
    feats = (jnp.maximum(pre, 0.0) * fmask).astype(jnp.bfloat16)
    width = w_dec.shape[2]
    n_targets = w_dec.shape[1]
    w_flat = w_dec.reshape(feat_dev, n_targets * width)
    tgt = targets.reshape(tok_rows, n_targets * width)
    if own:
        feats = by_owner(feats)
        err_all = exchange(feats, w_flat, tgt)
    else:
        recon = lax.psum_scatter(
            jnp.dot(feats, w_flat, preferred_element_type=jnp.float32),
            "layer",
            scatter_dimension=0,
            tiled=True,
        )
        err = (recon - tgt.astype(jnp.float32)).astype(jnp.bfloat16)
        err_all = lax.all_gather(err, "layer", axis=0, tiled=True)
    grad_dec = jnp.stack(
        [
            (
                lax.dot_general(
                    feats,
                    err_all[:, t * width : (t + 1) * width],
                    (((0,), (0,)), ((), ())),
                    preferred_element_type=jnp.float32,
                )
                * scale
            ).astype(jnp.bfloat16)
            for t in range(n_targets)
        ],
        axis=1,
    )
    gfeat = lax.dot_general(
        err_all, w_flat, (((1,), (1,)), ((), ())), preferred_element_type=jnp.float32
    ) * (feats > 0)
    grad_bias = jnp.sum(gfeat, axis=0) * scale
    gfeat_b = gfeat.astype(jnp.bfloat16)
    if own:
        gfeat_b = by_owner(gfeat_b, back=True)
    grad_enc = (
        lax.dot_general(
            inputs,
            gfeat_b,
            (((0,), (0,)), ((), ())),
            preferred_element_type=jnp.float32,
        )
        * scale
    ).astype(jnp.bfloat16)
    return (grad_enc, grad_bias, grad_dec)


def solution(mesh):
    placed = (
        P("groups", None),
        P(("groups", "layer"), None, None),
        P(None, "layer"),
        P("layer"),
        P("layer", None, None),
        P(),
    )
    return jax.shard_map(
        functools.partial(local, layers=mesh.shape["layer"]),
        mesh=mesh,
        in_specs=placed,
        out_specs=(
            P("groups", "layer"),
            P(("groups", "layer")),
            P(("groups", "layer"), None, None),
        ),
        check_vma=False,
    )
```

```python
import functools
import math

import jax
import jax.numpy as jnp
from jax import lax
from jax.experimental import pallas as pl
from jax.experimental.pallas import tpu as pltpu
from jax.sharding import PartitionSpec as P

TILE = 128
ZN, YN, CN = 4, 2, 2
PEERS = 5
STRIP = 256
CORE, YRS, ZRS, ZAG, YAG, CAG, KINDS = 0, 1, 2, 5, 8, 9, 10
LAG = (1, 3, 5, 7, 9, 10)


def exchange_kernel(
    chunks, scale, feats, w_hbm, tgt, gfeat, gdec, out, wbuf, part, r_core, r_y, r_z, feats_t, held,
    w_sem, send, recv, out_sem,
):
    me = lax.axis_index("layer")
    z, y, c = me // 4, (me // 2) % 2, me % 2
    rows = tgt.shape[0]
    quad, half = ZN * rows, YN * ZN * rows
    width = w_hbm.shape[1] // chunks
    core_peer = z * 4 + y * 2 + (1 - c)
    y_peer = z * 4 + (1 - y) * 2 + c
    z_of = [(z + d) % ZN for d in range(1, ZN)]
    z_from = [(z + ZN - d) % ZN for d in range(1, ZN)]
    z_peer = [zz * 4 + y * 2 + c for zz in z_of]

    def at(k):
        return pl.ds(pl.multiple_of(k * width, 128), width)

    def span(start, size):
        return pl.ds(pl.multiple_of(start, 32), size)

    own_half, far_half = span(c * half, half), span((1 - c) * half, half)
    own_quad = span(c * half + y * quad, quad)
    far_quad = span(c * half + (1 - y) * quad, quad)
    own = span(c * half + y * quad + z * rows, rows)

    def of_z(zz):
        return span(c * half + y * quad + zz * rows, rows)

    def copy(src, dst, kind, k, peer):
        return pltpu.make_async_remote_copy(
            src_ref=src,
            dst_ref=dst,
            send_sem=send.at[kind, k],
            recv_sem=recv.at[kind, k],
            device_id={"layer": peer},
            device_id_type=pl.DeviceIdType.MESH,
        )

    def load(k):
        return pltpu.make_async_copy(w_hbm.at[:, at(k)], wbuf.at[:, at(k)], w_sem.at[k])

    def store(k):
        per = gdec.shape[3] // width
        dst = gdec.at[:, k // per, :, pl.ds(pl.multiple_of((k % per) * width, 128), width)]
        return pltpu.make_async_copy(held.at[k % 2], dst, out_sem.at[k % 2])

    def core_copy(k):
        return copy(part.at[far_half, at(k)], r_core.at[:, at(k)], CORE, k, core_peer)

    def y_copy(k):
        return copy(part.at[far_quad, at(k)], r_y.at[:, at(k)], YRS, k, y_peer)

    def z_copy(k, d):
        return copy(part.at[of_z(z_of[d]), at(k)], r_z.at[d, :, at(k)], ZRS + d, k, z_peer[d])

    def z_send(k, d):
        return copy(out.at[own, at(k)], out.at[own, at(k)], ZAG + d, k, z_peer[d])

    def z_take(k, d):
        got = out.at[of_z(z_from[d]), at(k)]
        return copy(got, got, ZAG + d, k, z_peer[d])

    def y_send(k):
        return copy(out.at[own_quad, at(k)], out.at[own_quad, at(k)], YAG, k, y_peer)

    def y_take(k):
        got = out.at[far_quad, at(k)]
        return copy(got, got, YAG, k, y_peer)

    def core_send(k):
        return copy(out.at[own_half, at(k)], out.at[own_half, at(k)], CAG, k, core_peer)

    def core_take(k):
        got = out.at[far_half, at(k)]
        return copy(got, got, CAG, k, core_peer)

    barrier = pltpu.get_barrier_semaphore()
    for peer in (core_peer, y_peer, *z_peer):
        pl.semaphore_signal(
            barrier, inc=1, device_id={"layer": peer}, device_id_type=pl.DeviceIdType.MESH
        )

    @pl.loop(0, chunks)
    def _(k):
        load(k).start()

    feats_t[...] = feats[...].T
    gfeat[...] = jnp.zeros_like(gfeat)
    pl.semaphore_wait(barrier, PEERS)

    @pl.loop(0, chunks + LAG[-1])
    def _(s):
        @pl.when(s < chunks)
        def _():
            k = s
            load(k).wait()
            part[:, at(k)] = jnp.dot(
                feats[...], wbuf[:, at(k)], preferred_element_type=jnp.float32
            ).astype(jnp.bfloat16)
            core_copy(k).start()

        def stage(lag, body):
            @pl.when((s >= lag) & (s < lag + chunks))
            def _():
                body(s - lag)

        def after_core(k):
            core_copy(k).wait_recv()
            part[own_half, at(k)] = (
                part[own_half, at(k)].astype(jnp.float32) + r_core[:, at(k)].astype(jnp.float32)
            ).astype(jnp.bfloat16)
            y_copy(k).start()

        def after_y(k):
            y_copy(k).wait_recv()
            part[own_quad, at(k)] = (
                part[own_quad, at(k)].astype(jnp.float32) + r_y[:, at(k)].astype(jnp.float32)
            ).astype(jnp.bfloat16)
            for d in range(ZN - 1):
                z_copy(k, d).start()

        def after_z(k):
            total = part[own, at(k)].astype(jnp.float32)
            for d in range(ZN - 1):
                z_copy(k, d).wait_recv()
                total += r_z[d, :, at(k)].astype(jnp.float32)
            out[own, at(k)] = (total - tgt[:, at(k)].astype(jnp.float32)).astype(jnp.bfloat16)
            for d in range(ZN - 1):
                z_send(k, d).start()

        def after_zag(k):
            for d in range(ZN - 1):
                z_take(k, d).wait_recv()
            y_send(k).start()

        def after_yag(k):
            y_take(k).wait_recv()
            core_send(k).start()

        def after_cag(k):
            core_take(k).wait_recv()

            @pl.when(k >= 2)
            def _():
                store(k - 2).wait()

            @pl.loop(0, feats.shape[1] // STRIP)
            def _(j):
                strip = pl.ds(pl.multiple_of(j * STRIP, STRIP), STRIP)
                grad = jnp.dot(
                    feats_t[strip, :], out[:, at(k)], preferred_element_type=jnp.float32
                )
                held[k % 2, pl.ds(j * (STRIP // 8), STRIP // 8)] = (
                    (grad * scale).reshape(STRIP // 8, 8, width).astype(jnp.bfloat16)
                )
                gfeat[:, strip] += lax.dot_general(
                    out[:, at(k)],
                    wbuf[strip, at(k)],
                    (((1,), (1,)), ((), ())),
                    preferred_element_type=jnp.float32,
                )

            store(k).start()

        for lag, body in zip(
            LAG, (after_core, after_y, after_z, after_zag, after_yag, after_cag)
        ):
            stage(lag, body)

    for k in (chunks - 2, chunks - 1):
        store(k).wait()

    @pl.loop(0, chunks)
    def _(k):
        core_copy(k).wait_send()
        y_copy(k).wait_send()
        for d in range(ZN - 1):
            z_copy(k, d).wait_send()
            z_send(k, d).wait_send()
        y_send(k).wait_send()
        core_send(k).wait_send()


def exchange(feats, w_flat, tgt, targets, scale):
    tokens, depth = feats.shape
    columns = w_flat.shape[1]
    rows = tgt.shape[0]
    chunks = 14
    return pl.pallas_call(
        functools.partial(exchange_kernel, chunks, scale),
        out_shape=(
            jax.ShapeDtypeStruct((tokens, depth), jnp.float32),
            jax.ShapeDtypeStruct((depth // 8, targets, 8, columns // targets), jnp.bfloat16),
        ),
        in_specs=[
            pl.BlockSpec(memory_space=pltpu.VMEM),
            pl.BlockSpec(memory_space=pl.ANY),
            pl.BlockSpec(memory_space=pltpu.VMEM),
        ],
        out_specs=(pl.BlockSpec(memory_space=pltpu.VMEM), pl.BlockSpec(memory_space=pl.ANY)),
        scratch_shapes=[
            pltpu.VMEM((tokens, columns), jnp.bfloat16),
            pltpu.VMEM((depth, columns), jnp.bfloat16),
            pltpu.VMEM((tokens, columns), jnp.bfloat16),
            pltpu.VMEM((tokens // CN, columns), jnp.bfloat16),
            pltpu.VMEM((tokens // CN // YN, columns), jnp.bfloat16),
            pltpu.VMEM((ZN - 1, rows, columns), jnp.bfloat16),
            pltpu.VMEM((depth, tokens), jnp.bfloat16),
            pltpu.VMEM((2, depth // 8, 8, columns // chunks), jnp.bfloat16),
            pltpu.SemaphoreType.DMA((chunks,)),
            pltpu.SemaphoreType.DMA((KINDS, chunks)),
            pltpu.SemaphoreType.DMA((KINDS, chunks)),
            pltpu.SemaphoreType.DMA((2,)),
        ],
        compiler_params=pltpu.CompilerParams(
            collective_id=0, has_side_effects=True, vmem_limit_bytes=58 * 2**20
        ),
        cost_estimate=pl.CostEstimate(
            flops=6 * tokens * depth * columns,
            bytes_accessed=2 * (2 * depth + tokens) * columns,
            transcendentals=0,
        ),
    )(feats, w_flat, tgt)


def enc_grad(inputs, gfeat, scale):
    tokens, d = inputs.shape
    f = gfeat.shape[1]

    def body(x, g, o):
        o[...] = (
            lax.dot_general(
                x[...], g[...], (((0,), (0,)), ((), ())), preferred_element_type=jnp.float32
            )
            * scale
        ).astype(jnp.bfloat16)

    return pl.pallas_call(
        body,
        grid=(d // 512,),
        out_shape=jax.ShapeDtypeStruct((d, f), jnp.bfloat16),
        in_specs=[
            pl.BlockSpec((tokens, 512), lambda i: (0, i)),
            pl.BlockSpec((tokens, f), lambda i: (0, 0)),
        ],
        out_specs=pl.BlockSpec((512, f), lambda i: (i, 0)),
        compiler_params=pltpu.CompilerParams(vmem_limit_bytes=32 * 2**20),
    )(inputs, gfeat)


def by_owner(a, back=False):
    rows = a.shape[0] // (ZN * YN * CN)
    dims = (CN, YN, ZN) if back else (ZN, YN, CN)
    return a.reshape(*dims, rows, -1).transpose(2, 1, 0, 3, 4).reshape(a.shape)


def local(inputs, targets, w_enc, b_enc, w_dec, active_tiles, layers):
    total = inputs.shape[0]
    tok_rows = targets.shape[0]
    feat_dev = w_enc.shape[1]
    scale = 1.0 / math.sqrt(total)
    tiles_dev = feat_dev // TILE
    local_ids = lax.axis_index("layer") * tiles_dev + jnp.arange(tiles_dev, dtype=jnp.int32)
    tile_on = jnp.any(active_tiles[:, None] == local_ids[None, :], axis=0)
    fmask = jnp.repeat(tile_on, TILE).astype(jnp.float32)
    own = layers == ZN * YN * CN
    pre = jnp.dot(inputs, w_enc, preferred_element_type=jnp.float32) + b_enc
    feats = (jnp.maximum(pre, 0.0) * fmask).astype(jnp.bfloat16)
    width = w_dec.shape[2]
    n_targets = w_dec.shape[1]
    w_flat = w_dec.reshape(feat_dev, n_targets * width)
    tgt = targets.reshape(tok_rows, n_targets * width)
    if own:
        feats = by_owner(feats)
        gfeat, gdec = exchange(feats, w_flat, tgt, n_targets, scale)
        grad_dec = gdec.transpose(0, 2, 1, 3).reshape(w_dec.shape)
    else:
        recon = lax.psum_scatter(
            jnp.dot(feats, w_flat, preferred_element_type=jnp.float32),
            "layer",
            scatter_dimension=0,
            tiled=True,
        )
        err = (recon - tgt.astype(jnp.float32)).astype(jnp.bfloat16)
        err_all = lax.all_gather(err, "layer", axis=0, tiled=True)
        grad_dec = (
            lax.dot_general(
                feats, err_all, (((0,), (0,)), ((), ())), preferred_element_type=jnp.float32
            )
            * scale
        ).astype(jnp.bfloat16).reshape(w_dec.shape)
        gfeat = lax.dot_general(
            err_all, w_flat, (((1,), (1,)), ((), ())), preferred_element_type=jnp.float32
        )
    gfeat = gfeat * (feats > 0)
    grad_bias = jnp.sum(gfeat, axis=0) * scale
    gfeat_b = gfeat.astype(jnp.bfloat16)
    if own:
        gfeat_b = by_owner(gfeat_b, back=True)
    grad_enc = enc_grad(inputs, gfeat_b, scale)
    return (grad_enc, grad_bias, grad_dec)


def solution(mesh):
    placed = (
        P("groups", None),
        P(("groups", "layer"), None, None),
        P(None, "layer"),
        P("layer"),
        P("layer", None, None),
        P(),
    )
    return jax.shard_map(
        functools.partial(local, layers=mesh.shape["layer"]),
        mesh=mesh,
        in_specs=placed,
        out_specs=(
            P("groups", "layer"),
            P(("groups", "layer")),
            P(("groups", "layer"), None, None),
        ),
        check_vma=False,
    )
```

```python
import functools
import math

import jax
import jax.numpy as jnp
from jax import lax
from jax.experimental import pallas as pl
from jax.experimental.pallas import tpu as pltpu
from jax.sharding import PartitionSpec as P

TILE = 128
ZN, YN, CN = 4, 2, 2
PEERS = 5
STRIP = 256
CORE, YRS, ZRS, ZAG, YAG, CAG, KINDS = 0, 1, 2, 5, 8, 9, 10
LAG = (1, 3, 5, 7, 9, 10)


def exchange_kernel(
    chunks, scale, feats, w_hbm, tgt, gfeat, gdec, out, wbuf, part, r_core, r_y, r_z, feats_t, held,
    w_sem, send, recv, out_sem,
):
    me = lax.axis_index("layer")
    z, y, c = me // 4, (me // 2) % 2, me % 2
    rows = tgt.shape[0]
    quad, half = ZN * rows, YN * ZN * rows
    width = w_hbm.shape[1] // chunks
    core_peer = z * 4 + y * 2 + (1 - c)
    y_peer = z * 4 + (1 - y) * 2 + c
    z_of = [(z + d) % ZN for d in range(1, ZN)]
    z_from = [(z + ZN - d) % ZN for d in range(1, ZN)]
    z_peer = [zz * 4 + y * 2 + c for zz in z_of]

    def at(k):
        return pl.ds(pl.multiple_of(k * width, 128), width)

    def span(start, size):
        return pl.ds(pl.multiple_of(start, 32), size)

    own_half, far_half = span(c * half, half), span((1 - c) * half, half)
    own_quad = span(c * half + y * quad, quad)
    far_quad = span(c * half + (1 - y) * quad, quad)
    own = span(c * half + y * quad + z * rows, rows)

    def of_z(zz):
        return span(c * half + y * quad + zz * rows, rows)

    def copy(src, dst, kind, k, peer):
        return pltpu.make_async_remote_copy(
            src_ref=src,
            dst_ref=dst,
            send_sem=send.at[kind, k],
            recv_sem=recv.at[kind, k],
            device_id={"layer": peer},
            device_id_type=pl.DeviceIdType.MESH,
        )

    def load(k):
        return pltpu.make_async_copy(w_hbm.at[:, at(k)], wbuf.at[:, at(k)], w_sem.at[k])

    def store(k):
        return pltpu.make_async_copy(held.at[k % 2], gdec.at[:, at(k)], out_sem.at[k % 2])

    def core_copy(k):
        return copy(part.at[far_half, at(k)], r_core.at[:, at(k)], CORE, k, core_peer)

    def y_copy(k):
        return copy(part.at[far_quad, at(k)], r_y.at[:, at(k)], YRS, k, y_peer)

    def z_copy(k, d):
        return copy(part.at[of_z(z_of[d]), at(k)], r_z.at[d, :, at(k)], ZRS + d, k, z_peer[d])

    def z_send(k, d):
        return copy(out.at[own, at(k)], out.at[own, at(k)], ZAG + d, k, z_peer[d])

    def z_take(k, d):
        got = out.at[of_z(z_from[d]), at(k)]
        return copy(got, got, ZAG + d, k, z_peer[d])

    def y_send(k):
        return copy(out.at[own_quad, at(k)], out.at[own_quad, at(k)], YAG, k, y_peer)

    def y_take(k):
        got = out.at[far_quad, at(k)]
        return copy(got, got, YAG, k, y_peer)

    def core_send(k):
        return copy(out.at[own_half, at(k)], out.at[own_half, at(k)], CAG, k, core_peer)

    def core_take(k):
        got = out.at[far_half, at(k)]
        return copy(got, got, CAG, k, core_peer)

    barrier = pltpu.get_barrier_semaphore()
    for peer in (core_peer, y_peer, *z_peer):
        pl.semaphore_signal(
            barrier, inc=1, device_id={"layer": peer}, device_id_type=pl.DeviceIdType.MESH
        )

    @pl.loop(0, chunks)
    def _(k):
        load(k).start()

    feats_t[...] = feats[...].T
    gfeat[...] = jnp.zeros_like(gfeat)
    pl.semaphore_wait(barrier, PEERS)

    @pl.loop(0, chunks + LAG[-1])
    def _(s):
        @pl.when(s < chunks)
        def _():
            k = s
            load(k).wait()
            part[:, at(k)] = jnp.dot(
                feats[...], wbuf[:, at(k)], preferred_element_type=jnp.float32
            ).astype(jnp.bfloat16)
            core_copy(k).start()

        def stage(lag, body):
            @pl.when((s >= lag) & (s < lag + chunks))
            def _():
                body(s - lag)

        def after_core(k):
            core_copy(k).wait_recv()
            part[own_half, at(k)] = (
                part[own_half, at(k)].astype(jnp.float32) + r_core[:, at(k)].astype(jnp.float32)
            ).astype(jnp.bfloat16)
            y_copy(k).start()

        def after_y(k):
            y_copy(k).wait_recv()
            part[own_quad, at(k)] = (
                part[own_quad, at(k)].astype(jnp.float32) + r_y[:, at(k)].astype(jnp.float32)
            ).astype(jnp.bfloat16)
            for d in range(ZN - 1):
                z_copy(k, d).start()

        def after_z(k):
            total = part[own, at(k)].astype(jnp.float32)
            for d in range(ZN - 1):
                z_copy(k, d).wait_recv()
                total += r_z[d, :, at(k)].astype(jnp.float32)
            out[own, at(k)] = (total - tgt[:, at(k)].astype(jnp.float32)).astype(jnp.bfloat16)
            for d in range(ZN - 1):
                z_send(k, d).start()

        def after_zag(k):
            for d in range(ZN - 1):
                z_take(k, d).wait_recv()
            y_send(k).start()

        def after_yag(k):
            y_take(k).wait_recv()
            core_send(k).start()

        def after_cag(k):
            core_take(k).wait_recv()

            @pl.when(k >= 2)
            def _():
                store(k - 2).wait()

            @pl.loop(0, feats.shape[1] // STRIP)
            def _(j):
                strip = pl.ds(pl.multiple_of(j * STRIP, STRIP), STRIP)
                grad = jnp.dot(
                    feats_t[strip, :], out[:, at(k)], preferred_element_type=jnp.float32
                )
                held[k % 2, strip, :] = (grad * scale).astype(jnp.bfloat16)
                gfeat[:, strip] += lax.dot_general(
                    out[:, at(k)],
                    wbuf[strip, at(k)],
                    (((1,), (1,)), ((), ())),
                    preferred_element_type=jnp.float32,
                )

            store(k).start()

        for lag, body in zip(
            LAG, (after_core, after_y, after_z, after_zag, after_yag, after_cag)
        ):
            stage(lag, body)

    for k in (chunks - 2, chunks - 1):
        store(k).wait()

    @pl.loop(0, chunks)
    def _(k):
        core_copy(k).wait_send()
        y_copy(k).wait_send()
        for d in range(ZN - 1):
            z_copy(k, d).wait_send()
            z_send(k, d).wait_send()
        y_send(k).wait_send()
        core_send(k).wait_send()


def exchange(feats, w_flat, tgt, scale):
    tokens, depth = feats.shape
    columns = w_flat.shape[1]
    rows = tgt.shape[0]
    chunks = 14
    return pl.pallas_call(
        functools.partial(exchange_kernel, chunks, scale),
        out_shape=(
            jax.ShapeDtypeStruct((tokens, depth), jnp.float32),
            jax.ShapeDtypeStruct((depth, columns), jnp.bfloat16),
        ),
        in_specs=[
            pl.BlockSpec(memory_space=pltpu.VMEM),
            pl.BlockSpec(memory_space=pl.ANY),
            pl.BlockSpec(memory_space=pltpu.VMEM),
        ],
        out_specs=(pl.BlockSpec(memory_space=pltpu.VMEM), pl.BlockSpec(memory_space=pl.ANY)),
        scratch_shapes=[
            pltpu.VMEM((tokens, columns), jnp.bfloat16),
            pltpu.VMEM((depth, columns), jnp.bfloat16),
            pltpu.VMEM((tokens, columns), jnp.bfloat16),
            pltpu.VMEM((tokens // CN, columns), jnp.bfloat16),
            pltpu.VMEM((tokens // CN // YN, columns), jnp.bfloat16),
            pltpu.VMEM((ZN - 1, rows, columns), jnp.bfloat16),
            pltpu.VMEM((depth, tokens), jnp.bfloat16),
            pltpu.VMEM((2, depth, columns // chunks), jnp.bfloat16),
            pltpu.SemaphoreType.DMA((chunks,)),
            pltpu.SemaphoreType.DMA((KINDS, chunks)),
            pltpu.SemaphoreType.DMA((KINDS, chunks)),
            pltpu.SemaphoreType.DMA((2,)),
        ],
        compiler_params=pltpu.CompilerParams(
            collective_id=0, has_side_effects=True, vmem_limit_bytes=58 * 2**20
        ),
        cost_estimate=pl.CostEstimate(
            flops=6 * tokens * depth * columns,
            bytes_accessed=2 * (2 * depth + tokens) * columns,
            transcendentals=0,
        ),
    )(feats, w_flat, tgt)


def enc_grad(inputs, gfeat, scale):
    tokens, d = inputs.shape
    f = gfeat.shape[1]

    def body(x, g, o):
        o[...] = (
            lax.dot_general(
                x[...], g[...], (((0,), (0,)), ((), ())), preferred_element_type=jnp.float32
            )
            * scale
        ).astype(jnp.bfloat16)

    return pl.pallas_call(
        body,
        grid=(d // 512,),
        out_shape=jax.ShapeDtypeStruct((d, f), jnp.bfloat16),
        in_specs=[
            pl.BlockSpec((tokens, 512), lambda i: (0, i)),
            pl.BlockSpec((tokens, f), lambda i: (0, 0)),
        ],
        out_specs=pl.BlockSpec((512, f), lambda i: (i, 0)),
        compiler_params=pltpu.CompilerParams(vmem_limit_bytes=32 * 2**20),
    )(inputs, gfeat)


def by_target(flat, tile_on, targets):
    features, columns = flat.shape
    width = columns // targets
    block = 512
    steps = width // block

    def body(on, *refs):
        o = refs[-1]

        @pl.when(on[pl.program_id(0)] != 0)
        def _():
            for t in range(targets):
                o[:, t, :] = refs[t][...]

        @pl.when(on[pl.program_id(0)] == 0)
        def _():
            o[...] = jnp.zeros_like(o)

    return pl.pallas_call(
        body,
        out_shape=jax.ShapeDtypeStruct((features, targets, width), flat.dtype),
        grid_spec=pltpu.PrefetchScalarGridSpec(
            num_scalar_prefetch=1,
            grid=(features // TILE, steps),
            in_specs=[
                pl.BlockSpec((TILE, block), lambda i, j, on, t=t: (i, t * steps + j))
                for t in range(targets)
            ],
            out_specs=pl.BlockSpec((TILE, targets, block), lambda i, j, on: (i, 0, j)),
        ),
        compiler_params=pltpu.CompilerParams(vmem_limit_bytes=32 * 2**20),
    )(tile_on, *[flat] * targets)


def by_owner(a, back=False):
    rows = a.shape[0] // (ZN * YN * CN)
    dims = (CN, YN, ZN) if back else (ZN, YN, CN)
    return a.reshape(*dims, rows, -1).transpose(2, 1, 0, 3, 4).reshape(a.shape)


def local(inputs, targets, w_enc, b_enc, w_dec, active_tiles, layers):
    total = inputs.shape[0]
    tok_rows = targets.shape[0]
    feat_dev = w_enc.shape[1]
    scale = 1.0 / math.sqrt(total)
    tiles_dev = feat_dev // TILE
    local_ids = lax.axis_index("layer") * tiles_dev + jnp.arange(tiles_dev, dtype=jnp.int32)
    tile_on = jnp.any(active_tiles[:, None] == local_ids[None, :], axis=0)
    fmask = jnp.repeat(tile_on, TILE).astype(jnp.float32)
    own = layers == ZN * YN * CN
    pre = jnp.dot(inputs, w_enc, preferred_element_type=jnp.float32) + b_enc
    feats = (jnp.maximum(pre, 0.0) * fmask).astype(jnp.bfloat16)
    width = w_dec.shape[2]
    n_targets = w_dec.shape[1]
    w_flat = w_dec.reshape(feat_dev, n_targets * width)
    tgt = targets.reshape(tok_rows, n_targets * width)
    if own:
        feats = by_owner(feats)
        gfeat, gdec = exchange(feats, w_flat, tgt, scale)
        grad_dec = by_target(gdec, tile_on.astype(jnp.int32), n_targets)
    else:
        recon = lax.psum_scatter(
            jnp.dot(feats, w_flat, preferred_element_type=jnp.float32),
            "layer",
            scatter_dimension=0,
            tiled=True,
        )
        err = (recon - tgt.astype(jnp.float32)).astype(jnp.bfloat16)
        err_all = lax.all_gather(err, "layer", axis=0, tiled=True)
        grad_dec = (
            lax.dot_general(
                feats, err_all, (((0,), (0,)), ((), ())), preferred_element_type=jnp.float32
            )
            * scale
        ).astype(jnp.bfloat16).reshape(w_dec.shape)
        gfeat = lax.dot_general(
            err_all, w_flat, (((1,), (1,)), ((), ())), preferred_element_type=jnp.float32
        )
    gfeat = gfeat * (feats > 0)
    grad_bias = jnp.sum(gfeat, axis=0) * scale
    gfeat_b = gfeat.astype(jnp.bfloat16)
    if own:
        gfeat_b = by_owner(gfeat_b, back=True)
    grad_enc = enc_grad(inputs, gfeat_b, scale)
    return (grad_enc, grad_bias, grad_dec)


def solution(mesh):
    placed = (
        P("groups", None),
        P(("groups", "layer"), None, None),
        P(None, "layer"),
        P("layer"),
        P("layer", None, None),
        P(),
    )
    return jax.shard_map(
        functools.partial(local, layers=mesh.shape["layer"]),
        mesh=mesh,
        in_specs=placed,
        out_specs=(
            P("groups", "layer"),
            P(("groups", "layer")),
            P(("groups", "layer"), None, None),
        ),
        check_vma=False,
    )
```

```python
import functools
import math

import jax
import jax.numpy as jnp
from jax import lax
from jax.experimental import pallas as pl
from jax.experimental.pallas import tpu as pltpu
from jax.sharding import PartitionSpec as P

TILE = 128
ZN, YN, CN = 4, 2, 2
PEERS = 5
STRIP = 256
CORE, YRS, ZRS, ZAG, YAG, CAG, KINDS = 0, 1, 2, 5, 8, 9, 10
LAG = (1, 3, 5, 7, 9, 10)


def exchange_kernel(
    chunks, scale, feats, w_hbm, tgt, gfeat, gdec, out, wbuf, part, r_core, r_y, r_z, feats_t, held,
    w_sem, send, recv, out_sem,
):
    me = lax.axis_index("layer")
    z, y, c = me // 4, (me // 2) % 2, me % 2
    rows = tgt.shape[0]
    quad, half = ZN * rows, YN * ZN * rows
    width = w_hbm.shape[1] // chunks
    core_peer = z * 4 + y * 2 + (1 - c)
    y_peer = z * 4 + (1 - y) * 2 + c
    z_of = [(z + d) % ZN for d in range(1, ZN)]
    z_from = [(z + ZN - d) % ZN for d in range(1, ZN)]
    z_peer = [zz * 4 + y * 2 + c for zz in z_of]

    def at(k):
        return pl.ds(pl.multiple_of(k * width, 128), width)

    def span(start, size):
        return pl.ds(pl.multiple_of(start, 32), size)

    own_half, far_half = span(c * half, half), span((1 - c) * half, half)
    own_quad = span(c * half + y * quad, quad)
    far_quad = span(c * half + (1 - y) * quad, quad)
    own = span(c * half + y * quad + z * rows, rows)

    def of_z(zz):
        return span(c * half + y * quad + zz * rows, rows)

    def copy(src, dst, kind, k, peer):
        return pltpu.make_async_remote_copy(
            src_ref=src,
            dst_ref=dst,
            send_sem=send.at[kind, k],
            recv_sem=recv.at[kind, k],
            device_id={"layer": peer},
            device_id_type=pl.DeviceIdType.MESH,
        )

    def load(k):
        return pltpu.make_async_copy(w_hbm.at[:, at(k)], wbuf.at[:, at(k)], w_sem.at[k])

    def store(k):
        return pltpu.make_async_copy(held.at[k % 2], gdec.at[:, at(k)], out_sem.at[k % 2])

    def core_copy(k):
        return copy(part.at[far_half, at(k)], r_core.at[:, at(k)], CORE, k, core_peer)

    def y_copy(k):
        return copy(part.at[far_quad, at(k)], r_y.at[:, at(k)], YRS, k, y_peer)

    def z_copy(k, d):
        return copy(part.at[of_z(z_of[d]), at(k)], r_z.at[d, :, at(k)], ZRS + d, k, z_peer[d])

    def z_send(k, d):
        return copy(out.at[own, at(k)], out.at[own, at(k)], ZAG + d, k, z_peer[d])

    def z_take(k, d):
        got = out.at[of_z(z_from[d]), at(k)]
        return copy(got, got, ZAG + d, k, z_peer[d])

    def y_send(k):
        return copy(out.at[own_quad, at(k)], out.at[own_quad, at(k)], YAG, k, y_peer)

    def y_take(k):
        got = out.at[far_quad, at(k)]
        return copy(got, got, YAG, k, y_peer)

    def core_send(k):
        return copy(out.at[own_half, at(k)], out.at[own_half, at(k)], CAG, k, core_peer)

    def core_take(k):
        got = out.at[far_half, at(k)]
        return copy(got, got, CAG, k, core_peer)

    barrier = pltpu.get_barrier_semaphore()
    for peer in (core_peer, y_peer, *z_peer):
        pl.semaphore_signal(
            barrier, inc=1, device_id={"layer": peer}, device_id_type=pl.DeviceIdType.MESH
        )

    @pl.loop(0, chunks)
    def _(k):
        load(k).start()

    feats_t[...] = feats[...].T
    gfeat[...] = jnp.zeros_like(gfeat)
    pl.semaphore_wait(barrier, PEERS)

    @pl.loop(0, chunks + LAG[-1])
    def _(s):
        @pl.when(s < chunks)
        def _():
            k = s
            load(k).wait()
            part[:, at(k)] = jnp.dot(
                feats[...], wbuf[:, at(k)], preferred_element_type=jnp.float32
            ).astype(jnp.bfloat16)
            core_copy(k).start()

        def stage(lag, body):
            @pl.when((s >= lag) & (s < lag + chunks))
            def _():
                body(s - lag)

        def after_core(k):
            core_copy(k).wait_recv()
            part[own_half, at(k)] = (
                part[own_half, at(k)].astype(jnp.float32) + r_core[:, at(k)].astype(jnp.float32)
            ).astype(jnp.bfloat16)
            y_copy(k).start()

        def after_y(k):
            y_copy(k).wait_recv()
            part[own_quad, at(k)] = (
                part[own_quad, at(k)].astype(jnp.float32) + r_y[:, at(k)].astype(jnp.float32)
            ).astype(jnp.bfloat16)
            for d in range(ZN - 1):
                z_copy(k, d).start()

        def after_z(k):
            total = part[own, at(k)].astype(jnp.float32)
            for d in range(ZN - 1):
                z_copy(k, d).wait_recv()
                total += r_z[d, :, at(k)].astype(jnp.float32)
            out[own, at(k)] = (total - tgt[:, at(k)].astype(jnp.float32)).astype(jnp.bfloat16)
            for d in range(ZN - 1):
                z_send(k, d).start()

        def after_zag(k):
            for d in range(ZN - 1):
                z_take(k, d).wait_recv()
            y_send(k).start()

        def after_yag(k):
            y_take(k).wait_recv()
            core_send(k).start()

        def after_cag(k):
            core_take(k).wait_recv()

            @pl.when(k >= 2)
            def _():
                store(k - 2).wait()

            @pl.loop(0, feats.shape[1] // STRIP)
            def _(j):
                strip = pl.ds(pl.multiple_of(j * STRIP, STRIP), STRIP)
                grad = jnp.dot(
                    feats_t[strip, :], out[:, at(k)], preferred_element_type=jnp.float32
                )
                held[k % 2, strip, :] = (grad * scale).astype(jnp.bfloat16)
                gfeat[:, strip] += lax.dot_general(
                    out[:, at(k)],
                    wbuf[strip, at(k)],
                    (((1,), (1,)), ((), ())),
                    preferred_element_type=jnp.float32,
                )

            store(k).start()

        for lag, body in zip(
            LAG, (after_core, after_y, after_z, after_zag, after_yag, after_cag)
        ):
            stage(lag, body)

    for k in (chunks - 2, chunks - 1):
        store(k).wait()

    @pl.loop(0, chunks)
    def _(k):
        core_copy(k).wait_send()
        y_copy(k).wait_send()
        for d in range(ZN - 1):
            z_copy(k, d).wait_send()
            z_send(k, d).wait_send()
        y_send(k).wait_send()
        core_send(k).wait_send()


def exchange(feats, w_flat, tgt, scale):
    tokens, depth = feats.shape
    columns = w_flat.shape[1]
    rows = tgt.shape[0]
    chunks = 14
    return pl.pallas_call(
        functools.partial(exchange_kernel, chunks, scale),
        out_shape=(
            jax.ShapeDtypeStruct((tokens, depth), jnp.float32),
            jax.ShapeDtypeStruct((depth, columns), jnp.bfloat16),
        ),
        in_specs=[
            pl.BlockSpec(memory_space=pltpu.VMEM),
            pl.BlockSpec(memory_space=pl.ANY),
            pl.BlockSpec(memory_space=pltpu.VMEM),
        ],
        out_specs=(pl.BlockSpec(memory_space=pltpu.VMEM), pl.BlockSpec(memory_space=pl.ANY)),
        scratch_shapes=[
            pltpu.VMEM((tokens, columns), jnp.bfloat16),
            pltpu.VMEM((depth, columns), jnp.bfloat16),
            pltpu.VMEM((tokens, columns), jnp.bfloat16),
            pltpu.VMEM((tokens // CN, columns), jnp.bfloat16),
            pltpu.VMEM((tokens // CN // YN, columns), jnp.bfloat16),
            pltpu.VMEM((ZN - 1, rows, columns), jnp.bfloat16),
            pltpu.VMEM((depth, tokens), jnp.bfloat16),
            pltpu.VMEM((2, depth, columns // chunks), jnp.bfloat16),
            pltpu.SemaphoreType.DMA((chunks,)),
            pltpu.SemaphoreType.DMA((KINDS, chunks)),
            pltpu.SemaphoreType.DMA((KINDS, chunks)),
            pltpu.SemaphoreType.DMA((2,)),
        ],
        compiler_params=pltpu.CompilerParams(
            collective_id=0, has_side_effects=True, vmem_limit_bytes=58 * 2**20
        ),
        cost_estimate=pl.CostEstimate(
            flops=6 * tokens * depth * columns,
            bytes_accessed=2 * (2 * depth + tokens) * columns,
            transcendentals=0,
        ),
    )(feats, w_flat, tgt)


def enc_grad(inputs, gfeat, scale):
    tokens, d = inputs.shape
    f = gfeat.shape[1]

    def body(x, g, o):
        o[...] = (
            lax.dot_general(
                x[...], g[...], (((0,), (0,)), ((), ())), preferred_element_type=jnp.float32
            )
            * scale
        ).astype(jnp.bfloat16)

    return pl.pallas_call(
        body,
        grid=(d // 512,),
        out_shape=jax.ShapeDtypeStruct((d, f), jnp.bfloat16),
        in_specs=[
            pl.BlockSpec((tokens, 512), lambda i: (0, i)),
            pl.BlockSpec((tokens, f), lambda i: (0, 0)),
        ],
        out_specs=pl.BlockSpec((512, f), lambda i: (i, 0)),
        compiler_params=pltpu.CompilerParams(vmem_limit_bytes=32 * 2**20),
    )(inputs, gfeat)


def by_target(flat, tile_on, targets):
    features, columns = flat.shape
    width = columns // targets
    block = 896
    steps = width // block

    def body(on, *refs):
        o = refs[-1]

        @pl.when(on[pl.program_id(0)] != 0)
        def _():
            for t in range(targets):
                o[:, t, :] = refs[t][...]

        @pl.when(on[pl.program_id(0)] == 0)
        def _():
            o[...] = jnp.zeros_like(o)

    return pl.pallas_call(
        body,
        out_shape=jax.ShapeDtypeStruct((features, targets, width), flat.dtype),
        grid_spec=pltpu.PrefetchScalarGridSpec(
            num_scalar_prefetch=1,
            grid=(features // TILE, steps),
            in_specs=[
                pl.BlockSpec((TILE, block), lambda i, j, on, t=t: (i, t * steps + j))
                for t in range(targets)
            ],
            out_specs=pl.BlockSpec((TILE, targets, block), lambda i, j, on: (i, 0, j)),
        ),
        compiler_params=pltpu.CompilerParams(vmem_limit_bytes=58 * 2**20),
    )(tile_on, *[flat] * targets)


def by_owner(a, back=False):
    rows = a.shape[0] // (ZN * YN * CN)
    dims = (CN, YN, ZN) if back else (ZN, YN, CN)
    return a.reshape(*dims, rows, -1).transpose(2, 1, 0, 3, 4).reshape(a.shape)


def local(inputs, targets, w_enc, b_enc, w_dec, active_tiles, layers):
    total = inputs.shape[0]
    tok_rows = targets.shape[0]
    feat_dev = w_enc.shape[1]
    scale = 1.0 / math.sqrt(total)
    tiles_dev = feat_dev // TILE
    local_ids = lax.axis_index("layer") * tiles_dev + jnp.arange(tiles_dev, dtype=jnp.int32)
    tile_on = jnp.any(active_tiles[:, None] == local_ids[None, :], axis=0)
    fmask = jnp.repeat(tile_on, TILE).astype(jnp.float32)
    own = layers == ZN * YN * CN
    pre = jnp.dot(inputs, w_enc, preferred_element_type=jnp.float32) + b_enc
    feats = (jnp.maximum(pre, 0.0) * fmask).astype(jnp.bfloat16)
    width = w_dec.shape[2]
    n_targets = w_dec.shape[1]
    w_flat = w_dec.reshape(feat_dev, n_targets * width)
    tgt = targets.reshape(tok_rows, n_targets * width)
    if own:
        feats = by_owner(feats)
        gfeat, gdec = exchange(feats, w_flat, tgt, scale)
        grad_dec = by_target(gdec, tile_on.astype(jnp.int32), n_targets)
    else:
        recon = lax.psum_scatter(
            jnp.dot(feats, w_flat, preferred_element_type=jnp.float32),
            "layer",
            scatter_dimension=0,
            tiled=True,
        )
        err = (recon - tgt.astype(jnp.float32)).astype(jnp.bfloat16)
        err_all = lax.all_gather(err, "layer", axis=0, tiled=True)
        grad_dec = (
            lax.dot_general(
                feats, err_all, (((0,), (0,)), ((), ())), preferred_element_type=jnp.float32
            )
            * scale
        ).astype(jnp.bfloat16).reshape(w_dec.shape)
        gfeat = lax.dot_general(
            err_all, w_flat, (((1,), (1,)), ((), ())), preferred_element_type=jnp.float32
        )
    gfeat = gfeat * (feats > 0)
    grad_bias = jnp.sum(gfeat, axis=0) * scale
    gfeat_b = gfeat.astype(jnp.bfloat16)
    if own:
        gfeat_b = by_owner(gfeat_b, back=True)
    grad_enc = enc_grad(inputs, gfeat_b, scale)
    return (grad_enc, grad_bias, grad_dec)


def solution(mesh):
    placed = (
        P("groups", None),
        P(("groups", "layer"), None, None),
        P(None, "layer"),
        P("layer"),
        P("layer", None, None),
        P(),
    )
    return jax.shard_map(
        functools.partial(local, layers=mesh.shape["layer"]),
        mesh=mesh,
        in_specs=placed,
        out_specs=(
            P("groups", "layer"),
            P(("groups", "layer")),
            P(("groups", "layer"), None, None),
        ),
        check_vma=False,
    )
```
